1024 devices in a mesh: row: 32 (over z_hi, y, core), col: 32 (over z_lo, x).
Axes of the slice: x: 4, y: 4, z: 32 (z_hi: 4, z_lo: 8; z = z_hi * 8 + z_lo), core: 2. Of those that a mesh axis runs over, the one named last changes fastest.
Arguments:
- a_blocks: bfloat16 [128, 4096, 128], P('row', 'col'), may hold values from -0.5 to 0.5
- a_coord: int32 [32, 128], P('row', 'col'), may hold values from 0 to 15, as said below
- a_count: int32 [32, 32], P('row', 'col'), may hold values from 1 to 4, as said below
- b_blocks: bfloat16 [128, 4096, 128], P('row', 'col'), may hold values from -6 to 6
- b_coord: int32 [32, 128], P('row', 'col'), may hold values from 0 to 15, as said below
- b_count: int32 [32, 32], P('row', 'col'), may hold values from 1 to 4, as said below
- c_pattern: int32 [128, 128], P('row', 'col'), may hold values 0 or 1
Outputs:
- product: bfloat16 [16384, 16384], P('row', 'col')
The draws below stay inside these ranges and needn't reach their ends.
Inputs may be any that keep to these rules, and one draw needn't show every extreme that they name: `a_coord`: in each panel the codes of all 4 slots are distinct. `b_coord`: in each panel the codes of all 4 slots are distinct. `a_count`: some panel is full. `b_count`: some panel is full.
All inputs are finite; a program needn't handle non-finite values. No bound on the sum of `c_pattern` on one device may be relied on, other than what follows from the above.
Results may differ from the reference program's by a relative error of at most 0.001.
Values may be sent and summed in bfloat16 or wider, within the bound.
A program may use at most 32 MiB of HBM per device.

```python
import jax
import jax.numpy as jnp
from jax import lax

BW = 128
BR = 4
NB = 4
STEPS = 4
N_ROW = 32
N_COL = 32


def draw_codes(key):
    keys = jax.random.split(key, N_ROW * N_COL)
    picks = jax.vmap(lambda one_key: jax.random.permutation(one_key, BR * BR)[:NB])(keys)
    return picks.reshape(N_ROW, N_COL * NB).astype(jnp.int32)


def draw_counts(key):
    first_key, second_key = jax.random.split(key)
    counts = jax.random.randint(first_key, (N_ROW * N_COL,), 1, NB + 1).astype(jnp.int32)
    full_at = jax.random.randint(second_key, (), 0, N_ROW * N_COL).astype(jnp.int32)
    counts = jnp.where(jnp.arange(N_ROW * N_COL, dtype=jnp.int32) == full_at, NB, counts)
    return counts.reshape(N_ROW, N_COL).astype(jnp.int32)


def draw_a_coord(key, part):
    key = jax.random.fold_in(key, 11)
    return draw_codes(key)


def draw_b_coord(key, part):
    key = jax.random.fold_in(key, 23)
    return draw_codes(key)


def draw_a_count(key, part):
    key = jax.random.fold_in(key, 37)
    return draw_counts(key)


def draw_b_count(key, part):
    key = jax.random.fold_in(key, 41)
    return draw_counts(key)


def plant(values, key, least, largest):
    longest = values.shape.index(max(values.shape))
    spots = []
    for shift in (0, 1):
        where = [jax.random.randint(jax.random.fold_in(key, axis), (), 0, length) for axis, length in enumerate(values.shape)]
        where[longest] = (where[longest] + shift) % values.shape[longest]
        spots.append(tuple(where))
    return values.at[spots[0]].set(least).at[spots[1]].set(largest)


def steps_of(own_key, dims, pieces, low, high):
    loudness, own = 1.0, jax.random.fold_in(own_key, 6)
    for axis_at, shards_of in pieces:
        steps = jnp.exp(jax.random.uniform(jax.random.fold_in(own, axis_at), (shards_of,), jnp.float32, low / len(pieces), high / len(pieces)))
        loudness = loudness * jnp.repeat(steps, dims[axis_at] // shards_of).reshape([-1 if axis == axis_at else 1 for axis in range(len(dims))])
    return loudness


def bell_draw(own_key, shape, scale, bound, cuts=(), kind=jnp.bfloat16):
    drawn = jax.random.normal(own_key, shape, jnp.float32) * scale
    if len(cuts) > 0:
        drawn = steps_of(own_key, shape, cuts, -0.22, 0.18) * drawn
    return jnp.clip(drawn, min=-bound, max=bound).astype(kind)


def setup_inputs(seed: int = 0) -> dict:
    splits = jax.random.split(jax.random.key(seed), 8)
    return {
        "a_blocks": bell_draw(splits[0], (N_ROW * NB, N_COL * BW, BW), BW ** -0.5, 0.5, ((0, 32), (1, 32))),
        "a_coord": draw_a_coord(jax.random.fold_in(splits[7], 71), 0),
        "a_count": draw_a_count(jax.random.fold_in(splits[7], 71), 0),
        "b_blocks": bell_draw(splits[3], (N_ROW * NB, N_COL * BW, BW), 1.0, 6.0, ((0, 32), (1, 32))),
        "b_coord": draw_b_coord(jax.random.fold_in(splits[7], 71), 0),
        "b_count": draw_b_count(jax.random.fold_in(splits[7], 71), 0),
        "c_pattern": plant((jax.random.randint(splits[6], (BR * N_ROW, BR * N_COL), 0, 4) < 3).astype(jnp.int32), jax.random.fold_in(splits[6], 1), 0, 1),
    }


def panel_product(a_blocks, a_code, a_live_count, b_blocks, b_code, b_live_count, pattern):
    width = pattern.shape[0]
    slots_a = jnp.arange(a_blocks.shape[0], dtype=jnp.int32)
    slots_b = jnp.arange(b_blocks.shape[0], dtype=jnp.int32)
    places = jnp.arange(width, dtype=jnp.int32)
    a_live = (slots_a < a_live_count).astype(jnp.float32)
    b_live = (slots_b < b_live_count).astype(jnp.float32)
    a_row = a_code // width
    a_col = a_code % width
    b_row = b_code // width
    b_col = b_code % width
    row_hot = (a_row[:, None] == places[None, :]).astype(jnp.float32) * a_live[:, None]
    col_hot = (b_col[:, None] == places[None, :]).astype(jnp.float32) * b_live[:, None]
    linked = (a_col[:, None] == b_row[None, :]).astype(jnp.float32)
    kept = jnp.dot(jnp.dot(row_hot, pattern.astype(jnp.float32), precision=lax.Precision.HIGHEST), col_hot.T, precision=lax.Precision.HIGHEST)
    weight = linked * kept
    products = jnp.einsum('aik,bkj->abij', a_blocks, b_blocks, preferred_element_type=jnp.float32)
    scaled = products * weight[:, :, None, None]
    partial_rows = jnp.einsum('ar,abij->rbij', row_hot, scaled, precision=lax.Precision.HIGHEST)
    return jnp.einsum('bc,rbij->ricj', col_hot, partial_rows, precision=lax.Precision.HIGHEST)


def reference(a_blocks, a_coord, a_count, b_blocks, b_coord, b_count, c_pattern):
    a_all = a_blocks.reshape(N_ROW, NB, N_COL, BW, BW)
    b_all = b_blocks.reshape(N_ROW, NB, N_COL, BW, BW)
    a_codes = a_coord.reshape(N_ROW, N_COL, NB)
    b_codes = b_coord.reshape(N_ROW, N_COL, NB)
    pattern_all = c_pattern.reshape(N_ROW, BR, N_COL, BR)
    span = BR * BW

    def one_device(device):
        row_at = device // N_COL
        col_at = device % N_COL
        pattern = pattern_all[row_at, :, col_at, :]
        total = jnp.zeros((BR, BW, BR, BW), jnp.float32)
        for step in range(STEPS):
            a_at = (row_at + col_at + step) % N_COL
            b_at = (row_at + col_at + step) % N_ROW
            total = total + panel_product(a_all[row_at, :, a_at], a_codes[row_at, a_at], a_count[row_at, a_at], b_all[b_at, :, col_at], b_codes[b_at, col_at], b_count[b_at, col_at], pattern)
        return total.reshape(span, span).astype(jnp.bfloat16)

    panels = lax.map(one_device, jnp.arange(N_ROW * N_COL, dtype=jnp.int32))
    return panels.reshape(N_ROW, N_COL, span, span).transpose(0, 2, 1, 3).reshape(N_ROW * span, N_COL * span)
```

```python
import jax
import jax.numpy as jnp
from jax import lax
from jax.experimental import pallas as pl
from jax.experimental.pallas import tpu as pltpu
from jax.sharding import PartitionSpec as P

MESH = pl.DeviceIdType.MESH
STEPS = 4
NB = 4
BR = 4
BW = 128
DEAD = NB


class Place:
    def __init__(self):
        self.i = i = lax.axis_index("row")
        self.j = j = lax.axis_index("col")
        self.w, self.x = w, x = j // 4, j % 4
        self.zh, self.pos = zh, pos = i // 8, i % 8

        ahead = i - x
        d1, d2 = (ahead + 3) // 4, (ahead + 6) // 4
        self.two = two = d1 != d2
        self.ha = (x - i + 32) % 4
        self.z1, self.z2 = z1, z2 = (w + d1) % 8, (w + d2) % 8
        g1, g2 = (w - d1 + 16) % 8, (w - d2 + 16) % 8
        self.g1, self.g2 = g1, g2
        need1, need2 = g1 != w, two & (g2 != w)
        self.send1 = need1 & ~(need2 & (g1 > w))
        self.send2 = need2 & ~(need1 & (g1 < w) & (g1 > 0))
        self.own1, self.own2 = z1 == w, two & (z2 == w)
        self.in1 = (z1 != w) & ~(two & (w > z1) & (w - 1 != z1))
        self.in2 = two & (z2 != w) & ~((w + 1 <= 7) & (w + 1 < z2))
        self.late1 = (z1 != w) & ~self.in1
        self.late2 = two & (z2 != w) & ~self.in2
        self.relay1 = two & (w >= 1) & (w < z1)
        self.relay2 = two & (w <= 6) & (w > z2)

        e = j - pos
        self.hb = (pos - j + 32) % 8
        minus = ((e >= -2) & (e <= 11)) | (e >= 30)
        plus = (e >= 12) & (e <= 24)
        self.hop1 = minus | plus
        self.hop2 = (e >= 6) & (e <= 16)
        self.b_to = ((zh + jnp.where(minus, 3, 1)) % 4) * 8 + pos
        self.b_from = ((zh + jnp.where(minus, 1, 3)) % 4) * 8 + pos
        self.first = jnp.where((e <= 0) | (e >= 25), 0, jnp.where((e >= 9) & (e <= 16), 2, 1))
        self.second = jnp.where(
            (e <= -3) | ((e >= 22) & (e <= 29)), 0, jnp.where((e >= 6) & (e <= 13), 2, 1)
        )

    def a_peer(self, turn):
        xd = (self.x + turn) % 4
        step = (self.x - self.i - xd + 64) % 4
        slot = jnp.where(xd <= self.ha, 0, 1)
        return (self.i, self.w * 4 + xd), step, slot

    def a_step_from(self, turn):
        return ((self.x + turn) - self.i - self.x + 64) % 4

    def b_peer(self, step):
        pd = (self.pos - self.j - step + 64) % 8
        slot = jnp.where(step <= self.hb, self.first, self.second)
        return (self.zh * 8 + pd, self.j), pd == self.pos, slot

    def b_source(self, step):
        ps = (self.pos + self.j + step) % 8
        return (self.zh * 8 + ps, self.j)

    def z_peer(self, z):
        return (self.i, z * 4 + self.x)


def live_table(coord, count):
    lane = lax.broadcasted_iota(jnp.int32, (8, 128), 1)
    table = jnp.full((8, 128), DEAD, jnp.int32)
    for s in range(NB):
        live = s < count[0, 0]
        table = jnp.where((lane == coord[0, s]) & live, s, table)
        table = jnp.where(lane == 16 + s, jnp.where(live, coord[0, s], -1), table)
    return table


def move_kernel(
    a_ref, b_ref, a_coord, a_count, b_coord, b_count,
    a_out, b_out, a_table_out, b_table_out,
    a_buf, b_buf, a_own_table, b_own_table, a_table, b_table,
    a_send, a_relay, a_fan, b_send, b_relay, b_fan,
    a_have, b_have, a_got, b_got,
):
    at = Place()
    i, w = at.i, at.w

    a_own_table[...] = live_table(a_coord, a_count)
    b_own_table[...] = live_table(b_coord, b_count)

    def a_own(p):
        return a_own_table if p is NB else a_ref.at[p]

    def b_own(p):
        return b_own_table if p is NB else b_ref.at[p]

    def a_slot(k, p):
        return a_table.at[k] if p is NB else a_buf.at[k, p]

    def b_slot(k, p):
        return b_table.at[k] if p is NB else b_buf.at[k, p]

    def a_final(s, p):
        return a_table_out.at[s] if p is NB else a_out.at[s, p]

    def b_final(s, p):
        return b_table_out.at[s] if p is NB else b_out.at[s, p]

    def remote(src, dst, send, recv, to):
        return pltpu.make_async_remote_copy(
            src_ref=src, dst_ref=dst, send_sem=send, recv_sem=recv, device_id=to, device_id_type=MESH
        )

    def a_direct(n, p):
        to = at.z_peer(at.g1 if n == 0 else at.g2)
        return remote(a_own(p), a_slot(n, p), a_send.at[n, p], a_have.at[n, p], to)

    def a_on(n, p):
        to = at.z_peer(at.w - 1 if n == 0 else at.w + 1)
        return remote(a_slot(n, p), a_slot(1 - n, p), a_relay.at[n, p], a_have.at[1 - n, p], to)

    def a_keep(n, p):
        return pltpu.make_async_copy(a_own(p), a_slot(n, p), a_have.at[n, p])

    def a_spread(turn, p):
        to, step, slot = at.a_peer(turn)
        if turn == 0:
            return pltpu.make_async_copy(a_slot(slot, p), a_final(step, p), a_got.at[step, p])
        return remote(a_slot(slot, p), a_final(step, p), a_fan.at[turn - 1, p], a_got.at[step, p], to)

    def b_direct(p):
        return remote(b_own(p), b_slot(1, p), b_send.at[p], b_have.at[1, p], (at.b_to, at.j))

    def b_on(p):
        return remote(b_slot(1, p), b_slot(2, p), b_relay.at[p], b_have.at[2, p], (at.b_to, at.j))

    def b_keep(p):
        return pltpu.make_async_copy(b_own(p), b_slot(0, p), b_have.at[0, p])

    def b_spread(step, p):
        to, _, slot = at.b_peer(step)
        return remote(b_slot(slot, p), b_final(step, p), b_fan.at[step, p], b_got.at[step, p], to)

    def b_spread_here(step, p):
        _, _, slot = at.b_peer(step)
        return pltpu.make_async_copy(b_slot(slot, p), b_final(step, p), b_got.at[step, p])

    barrier = pltpu.get_barrier_semaphore()

    def greet(device):
        pl.semaphore_signal(barrier, inc=1, device_id=device, device_id_type=MESH)

    def greet_if(cond, device):
        @pl.when(cond)
        def _():
            greet(device)

    def each_piece(body):
        body(NB)
        lax.fori_loop(0, NB, lambda p, c: (body(p), c)[1], 0)

    greet_if(at.in1, at.z_peer(at.z1))
    greet_if(at.in2, at.z_peer(at.z2))
    greet_if(at.late1, at.z_peer(at.w - 1))
    greet_if(at.late2, at.z_peer(at.w + 1))
    greet_if(at.hop1, (at.b_from, at.j))
    for turn in (1, 2, 3):
        greet((i, w * 4 + (at.x + turn) % 4))
    away = jnp.int32(0)
    for step in range(STEPS):
        _, here, _ = at.b_peer(step)
        source = at.b_source(step)
        greet_if(source[0] != i, source)
        away = away + jnp.where(here, 0, 1)

    def keep(p):
        @pl.when(at.own1)
        def _():
            a_keep(0, p).start()

        @pl.when(at.own2)
        def _():
            a_keep(1, p).start()

        b_keep(p).start()

    each_piece(keep)

    def one(flag):
        return jnp.where(flag, 1, 0)

    pl.semaphore_wait(
        barrier,
        3 + away + one(at.send1) + one(at.send2) + one(at.relay1) + one(at.relay2) + one(at.hop1),
    )

    def leave(p):
        @pl.when(at.hop1)
        def _():
            b_direct(p).start()

        @pl.when(at.send1)
        def _():
            a_direct(0, p).start()

        @pl.when(at.send2)
        def _():
            a_direct(1, p).start()

    each_piece(leave)

    def spread_a(p, slot_ready):
        for turn in (1, 2, 3, 0):
            _, _, slot = at.a_peer(turn)

            @pl.when(jnp.where(slot == 0, slot_ready[0], slot_ready[1]))
            def _():
                a_spread(turn, p).start()

    def spread_b(p, ready):
        for step in range(STEPS):
            _, here, slot = at.b_peer(step)

            @pl.when(ready(slot) & ~here)
            def _():
                b_spread(step, p).start()

            @pl.when(ready(slot) & here)
            def _():
                b_spread_here(step, p).start()

    early1, early2 = at.in1 | at.own1, at.in2 | at.own2

    def relay(p):
        b_keep(p).wait()

        @pl.when(at.hop1)
        def _():
            b_direct(p).wait_recv()

        @pl.when(at.hop2)
        def _():
            b_on(p).start()

        @pl.when(early1)
        def _():
            a_direct(0, p).wait_recv()

        @pl.when(at.relay1)
        def _():
            a_on(0, p).start()

        @pl.when(early2)
        def _():
            a_direct(1, p).wait_recv()

        @pl.when(at.relay2)
        def _():
            a_on(1, p).start()

        spread_b(p, lambda slot: slot <= 1)
        spread_a(p, (early1, early2))

    each_piece(relay)

    def late(p):
        @pl.when(at.late1)
        def _():
            a_direct(0, p).wait_recv()

        @pl.when(at.late2)
        def _():
            a_direct(1, p).wait_recv()

        spread_a(p, (at.late1, at.late2))

        @pl.when(at.hop2)
        def _():
            b_on(p).wait_recv()

        spread_b(p, lambda slot: slot == 2)

    each_piece(late)

    def finish(p):
        for step in range(STEPS):
            pltpu.make_async_copy(a_final(step, p), a_final(step, p), a_got.at[step, p]).wait()
            pltpu.make_async_copy(b_final(step, p), b_final(step, p), b_got.at[step, p]).wait()
        for turn in (1, 2, 3):
            a_spread(turn, p).wait_send()
        for step in range(STEPS):
            _, here, _ = at.b_peer(step)

            @pl.when(~here)
            def _():
                b_spread(step, p).wait_send()

        for cond, copy in (
            (at.send1, lambda: a_direct(0, p)),
            (at.send2, lambda: a_direct(1, p)),
            (at.relay1, lambda: a_on(0, p)),
            (at.relay2, lambda: a_on(1, p)),
            (at.hop1, lambda: b_direct(p)),
            (at.hop2, lambda: b_on(p)),
        ):

            @pl.when(cond)
            def _():
                copy().wait_send()

    each_piece(finish)


def move(a_blocks, b_blocks, a_coord, a_count, b_coord, b_count):
    pieces = NB + 1
    dma = pltpu.SemaphoreType.DMA
    panel = jax.ShapeDtypeStruct((STEPS, NB, BW, BW), jnp.bfloat16)
    table = jax.ShapeDtypeStruct((STEPS, 8, 128), jnp.int32)
    anywhere = pl.BlockSpec(memory_space=pl.ANY)
    scalars = pl.BlockSpec(memory_space=pltpu.SMEM)
    return pl.pallas_call(
        move_kernel,
        out_shape=[panel, panel, table, table],
        in_specs=[anywhere] * 2 + [scalars] * 4,
        out_specs=[anywhere] * 4,
        scratch_shapes=[
            pltpu.VMEM((2, NB, BW, BW), jnp.bfloat16),
            pltpu.VMEM((3, NB, BW, BW), jnp.bfloat16),
            pltpu.VMEM((8, 128), jnp.int32),
            pltpu.VMEM((8, 128), jnp.int32),
            pltpu.VMEM((2, 8, 128), jnp.int32),
            pltpu.VMEM((3, 8, 128), jnp.int32),
            dma((2, pieces)),
            dma((2, pieces)),
            dma((3, pieces)),
            dma((pieces,)),
            dma((pieces,)),
            dma((STEPS, pieces)),
            dma((2, pieces)),
            dma((3, pieces)),
            dma((STEPS, pieces)),
            dma((STEPS, pieces)),
        ],
        compiler_params=pltpu.CompilerParams(collective_id=0, has_side_effects=True),
    )(a_blocks, b_blocks, a_coord, a_count, b_coord, b_count)


def product_kernel(a_table, b_table, pattern, a_ref, b_ref, out_ref, total):
    total[...] = jnp.zeros_like(total)
    for step in range(STEPS):
        for slot in range(NB):
            code = a_table[step, 0, 16 + slot]

            @pl.when(code >= 0)
            def _():
                r, k = code // BR, code % BR
                blocks = []
                for c in range(BR):
                    which = b_table[step, 0, k * BR + c]
                    block = b_ref[step, jnp.minimum(which, NB - 1)]
                    kept = (which < NB) & (pattern[r, c] > 0)
                    blocks.append(jnp.where(kept, block, jnp.zeros_like(block)))
                row = jnp.concatenate(blocks, axis=1)
                total[r] += jnp.dot(a_ref[step, slot], row, preferred_element_type=jnp.float32)

    out_ref[...] = total[...].reshape(out_ref.shape).astype(out_ref.dtype)


def product(a_panels, b_panels, a_table, b_table, pattern):
    whole = pl.BlockSpec(memory_space=pltpu.VMEM)
    scalars = pl.BlockSpec(memory_space=pltpu.SMEM)
    span = BR * BW
    return pl.pallas_call(
        product_kernel,
        out_shape=jax.ShapeDtypeStruct((span, span), jnp.bfloat16),
        in_specs=[scalars] * 3 + [whole] * 2,
        out_specs=whole,
        scratch_shapes=[pltpu.VMEM((BR, BW, span), jnp.float32)],
    )(a_table, b_table, pattern, a_panels, b_panels)


def per_device(a_blocks, a_coord, a_count, b_blocks, b_coord, b_count, c_pattern):
    moved = move(a_blocks, b_blocks, a_coord, a_count, b_coord, b_count)
    return product(*moved, c_pattern)


def solution(mesh):
    placed = (
        P("row", "col", None),
        P("row", "col"),
        P("row", "col"),
        P("row", "col", None),
        P("row", "col"),
        P("row", "col"),
        P("row", "col"),
    )
    return jax.shard_map(
        per_device, mesh=mesh, in_specs=placed, out_specs=P("row", "col"), check_vma=False
    )
```

```python
import jax
import jax.numpy as jnp
from jax import lax
from jax.experimental import pallas as pl
from jax.experimental.pallas import tpu as pltpu
from jax.sharding import PartitionSpec as P

MESH = pl.DeviceIdType.MESH
STEPS = 4
NB = 4
BR = 4
BW = 128
DEAD = NB
NP = 4


class Place:
    def __init__(self):
        self.i = i = lax.axis_index("row")
        self.j = j = lax.axis_index("col")
        self.w, self.x = w, x = j // 4, j % 4
        self.zh, self.pos = zh, pos = i // 8, i % 8

        ahead = i - x
        d1, d2 = (ahead + 3) // 4, (ahead + 6) // 4
        self.two = two = d1 != d2
        self.ha = (x - i + 32) % 4
        self.z1, self.z2 = z1, z2 = (w + d1) % 8, (w + d2) % 8
        g1, g2 = (w - d1 + 16) % 8, (w - d2 + 16) % 8
        self.g1, self.g2 = g1, g2
        need1, need2 = g1 != w, two & (g2 != w)
        self.send1 = need1 & ~(need2 & (g1 > w))
        self.send2 = need2 & ~(need1 & (g1 < w) & (g1 > 0))
        self.own1, self.own2 = z1 == w, two & (z2 == w)
        self.in1 = (z1 != w) & ~(two & (w > z1) & (w - 1 != z1))
        self.in2 = two & (z2 != w) & ~((w + 1 <= 7) & (w + 1 < z2))
        self.late1 = (z1 != w) & ~self.in1
        self.late2 = two & (z2 != w) & ~self.in2
        self.relay1 = two & (w >= 1) & (w < z1)
        self.relay2 = two & (w <= 6) & (w > z2)

        e = j - pos
        self.hb = (pos - j + 32) % 8
        self.core, self.twin = pos % 2, (zh * 8 + pos + 1 - 2 * (pos % 2), j)
        down = ((e >= -2) & (e <= 8)) | (e >= 30)
        up = (e >= 14) & (e <= 24)
        self.near = near = down | up
        self.far = far = (e >= 6) & (e <= 16)
        self.near_to = jnp.where(down, (zh + 3) % 4, (zh + 1) % 4) * 8 + pos
        self.near_from = jnp.where(down, (zh + 1) % 4, (zh + 3) % 4) * 8 + pos
        self.far_to = ((zh + 2) % 4) * 8 + pos
        late = near & ~far
        greet_up = near & ((zh <= 1) | ((zh == 2) & ~late))
        greet_down = near & ((zh == 0) | ((zh == 3) & late))
        self.greet_to = jnp.where(down, greet_down, greet_up)
        self.greet_from = jnp.where(down, greet_up, greet_down)
        self.met_to, self.met_from = near & ~self.greet_to, near & ~self.greet_from
        self.greet_far, self.met_far = far & (zh <= 1), far & (zh >= 2)
        self.first = jnp.where((e <= 0) | (e >= 25), 0, jnp.where((e >= 9) & (e <= 16), 2, 1))
        self.second = jnp.where(
            (e <= -3) | ((e >= 22) & (e <= 29)), 0, jnp.where((e >= 6) & (e <= 13), 2, 1)
        )

    def a_peer(self, turn):
        xd = (self.x + turn) % 4
        step = (self.x - self.i - xd + 64) % 4
        slot = jnp.where(xd <= self.ha, 0, 1)
        return (self.i, self.w * 4 + xd), step, slot

    def a_step_from(self, turn):
        return ((self.x + turn) - self.i - self.x + 64) % 4

    def b_peer(self, step):
        pd = (self.pos - self.j - step + 64) % 8
        slot = jnp.where(step <= self.hb, self.first, self.second)
        return (self.zh * 8 + pd, self.j), pd == self.pos, slot

    def b_direct(self, step):
        return (self.pos - self.j) % 2 == 0 if step == 3 else step != 1

    def b_source(self, step):
        ps = (self.pos + self.j + step) % 8
        return (self.zh * 8 + ps, self.j)

    def z_peer(self, z):
        return (self.i, z * 4 + self.x)


def live_table(coord, count):
    lane = lax.broadcasted_iota(jnp.int32, (8, 128), 1)
    table = jnp.full((8, 128), DEAD, jnp.int32)
    for s in range(NB):
        live = s < count[0, 0]
        table = jnp.where((lane == coord[0, s]) & live, s, table)
        table = jnp.where(lane == 16 + s, jnp.where(live, coord[0, s], -1), table)
    return table


def move_kernel(
    a_ref, b_ref, a_coord, a_count, b_coord, b_count,
    a_out, b_out, a_table_out, b_table_out,
    a_buf, b_buf, a_own_table, b_own_table, a_table, b_table,
    a_send, a_relay, a_fan, b_send, b_fan, b_pass,
    a_have, b_have, a_got, b_got, near_ready, far_ready, below, above,
):
    at = Place()
    i, w = at.i, at.w

    a_own_table[...] = live_table(a_coord, a_count)
    b_own_table[...] = live_table(b_coord, b_count)

    def part(p):
        return pl.ds(p * (NB // NP), NB // NP)

    def a_own(p):
        return a_own_table if p is NB else a_ref.at[part(p)]

    def b_own(p):
        return b_own_table if p is NB else b_ref.at[part(p)]

    def a_slot(k, p):
        return a_table.at[k] if p is NB else a_buf.at[k, part(p)]

    def b_slot(k, p):
        return b_table.at[k] if p is NB else b_buf.at[k, part(p)]

    def a_final(s, p):
        return a_table_out.at[s] if p is NB else a_out.at[s, part(p)]

    def b_final(s, p):
        return b_table_out.at[s] if p is NB else b_out.at[s, part(p)]

    def remote(src, dst, send, recv, to):
        return pltpu.make_async_remote_copy(
            src_ref=src, dst_ref=dst, send_sem=send, recv_sem=recv, device_id=to, device_id_type=MESH
        )

    def a_direct(n, p):
        to = at.z_peer(at.g1 if n == 0 else at.g2)
        return remote(a_own(p), a_slot(n, p), a_send.at[n, p], a_have.at[n, p], to)

    def a_on(n, p):
        to = at.z_peer(at.w - 1 if n == 0 else at.w + 1)
        return remote(a_slot(n, p), a_slot(1 - n, p), a_relay.at[n, p], a_have.at[1 - n, p], to)

    def a_keep(n, p):
        return pltpu.make_async_copy(a_own(p), a_slot(n, p), a_have.at[n, p])

    def a_spread(turn, p):
        to, step, slot = at.a_peer(turn)
        if turn == 0:
            return pltpu.make_async_copy(a_slot(slot, p), a_final(step, p), a_got.at[step, p])
        return remote(a_slot(slot, p), a_final(step, p), a_fan.at[turn - 1, p], a_got.at[step, p], to)

    def b_near(p):
        return remote(b_own(p), b_slot(1, p), b_send.at[0, p], b_have.at[1, p], (at.near_to, at.j))

    def b_far(p):
        return remote(b_own(p), b_slot(2, p), b_send.at[1, p], b_have.at[2, p], (at.far_to, at.j))

    def b_keep(p):
        return pltpu.make_async_copy(b_own(p), b_slot(0, p), b_have.at[0, p])

    def b_spread(step, p):
        to, _, slot = at.b_peer(step)
        return remote(b_slot(slot, p), b_final(step, p), b_fan.at[step, p], b_got.at[step, p], to)

    def b_spread_here(step, p):
        _, _, slot = at.b_peer(step)
        return pltpu.make_async_copy(b_slot(slot, p), b_final(step, p), b_got.at[step, p])

    def b_twin(step, to, p):
        return remote(b_final(step, p), b_final(to, p), b_pass.at[to // 2, p], b_got.at[to, p], at.twin)

    def b_wait(step, p):
        pltpu.make_async_copy(b_final(step, p), b_final(step, p), b_got.at[step, p]).wait()

    barrier = pltpu.get_barrier_semaphore()

    def greet(device):
        pl.semaphore_signal(barrier, inc=1, device_id=device, device_id_type=MESH)

    def greet_if(cond, device):
        @pl.when(cond)
        def _():
            greet(device)

    def each_piece(body):
        body(NB)
        lax.fori_loop(0, NP, lambda p, c: (body(p), c)[1], 0)

    greet_if(w > 0, at.z_peer(w - 1))
    greet_if(w < 7, at.z_peer(w + 1))
    greet_if(at.greet_to, (at.near_to, at.j))
    greet_if(at.greet_from, (at.near_from, at.j))
    greet_if(at.greet_far, (at.far_to, at.j))
    for turn in (1, 2, 3):
        greet((i, w * 4 + (at.x + turn) % 4))
    greet(at.twin)
    away = jnp.int32(1)
    for step in (0, 2, 3):
        _, here, _ = at.b_peer(step)
        source = at.b_source(step)
        greet_if((source[0] != i) & ((at.core == 1) | (step != 3)), source)
        away = away + jnp.where(at.b_direct(step) & ~here, 1, 0)

    def keep(p):
        @pl.when(at.own1)
        def _():
            a_keep(0, p).start()

        @pl.when(at.own2)
        def _():
            a_keep(1, p).start()

        b_keep(p).start()

    each_piece(keep)

    def one(flag):
        return jnp.where(flag, 1, 0)

    pl.semaphore_wait(
        barrier,
        3 + away + one(w > 0) + one(w < 7) + one(at.met_to) + one(at.met_from) + one(at.met_far),
    )

    def leave_near(p):
        b_near(p).start()

    def leave_far(p):
        b_far(p).start()

    def leave_a(p):
        @pl.when(at.send1)
        def _():
            a_direct(0, p).start()

        @pl.when(at.send2)
        def _():
            a_direct(1, p).start()

    def spread_a(p, slot_ready):
        for turn in (1, 2, 3, 0):
            _, _, slot = at.a_peer(turn)

            @pl.when(jnp.where(slot == 0, slot_ready[0], slot_ready[1]))
            def _():
                a_spread(turn, p).start()

    def spread_b(p, ready):
        for step in (0, 2, 3):
            _, here, slot = at.b_peer(step)
            mine = ready(slot) & at.b_direct(step)

            @pl.when(mine & ~here)
            def _():
                b_spread(step, p).start()

            @pl.when(mine & here)
            def _():
                b_spread_here(step, p).start()

    early1, early2 = at.in1 | at.own1, at.in2 | at.own2

    def near_b(p):
        b_keep(p).wait()

        @pl.when(at.near)
        def _():
            b_near(p).wait_recv()

        spread_b(p, lambda slot: slot <= 1)

    def relay_a(p):
        @pl.when(early1)
        def _():
            a_direct(0, p).wait_recv()

        @pl.when(at.relay1)
        def _():
            a_on(0, p).start()

        @pl.when(early2)
        def _():
            a_direct(1, p).wait_recv()

        @pl.when(at.relay2)
        def _():
            a_on(1, p).start()

        spread_a(p, (early1, early2))

    def late_a(p):
        @pl.when(at.late1)
        def _():
            a_direct(0, p).wait_recv()

        @pl.when(at.late2)
        def _():
            a_direct(1, p).wait_recv()

        spread_a(p, (at.late1, at.late2))

    def far_b(p):
        @pl.when(at.far)
        def _():
            b_far(p).wait_recv()

        spread_b(p, lambda slot: slot == 2)

    @pl.when(at.met_from)
    def _():
        pl.semaphore_signal(near_ready, inc=1, device_id=(at.near_from, at.j), device_id_type=MESH)

    @pl.when(at.met_far)
    def _():
        pl.semaphore_signal(far_ready, inc=1, device_id=(at.far_to, at.j), device_id_type=MESH)

    @pl.when(at.met_far & (at.zh == 2))
    def _():
        each_piece(leave_far)

    @pl.when(at.met_to)
    def _():
        each_piece(leave_near)

    @pl.when(at.met_far & (at.zh == 3))
    def _():
        each_piece(leave_far)

    def from_below():
        @pl.when(w > 0)
        def _():
            pl.semaphore_wait(below, 1)

        @pl.when(w < 7)
        def _():
            pl.semaphore_signal(below, inc=1, device_id=at.z_peer(w + 1), device_id_type=MESH)

    def from_above():
        @pl.when(w < 7)
        def _():
            pl.semaphore_wait(above, 1)

        @pl.when(w > 0)
        def _():
            pl.semaphore_signal(above, inc=1, device_id=at.z_peer(w - 1), device_id_type=MESH)

    @pl.when(w < 4)
    def _():
        from_below()
        from_above()

    @pl.when(w >= 4)
    def _():
        from_above()
        from_below()

    each_piece(leave_a)
    a_first = at.zh == 0

    @pl.when(a_first)
    def _():
        each_piece(relay_a)
        each_piece(late_a)

    @pl.when(at.greet_to)
    def _():
        pl.semaphore_wait(near_ready, 1)
        each_piece(leave_near)

    @pl.when(at.greet_far)
    def _():
        pl.semaphore_wait(far_ready, 1)
        each_piece(leave_far)

    each_piece(near_b)

    @pl.when(~a_first)
    def _():
        each_piece(relay_a)
        each_piece(late_a)

    each_piece(far_b)

    def share(p):
        b_wait(0, p)

        @pl.when(at.core == 1)
        def _():
            b_twin(0, 1, p).start()

        b_wait(2, p)

        @pl.when(at.core == 1)
        def _():
            b_twin(2, 3, p).start()

        @pl.when(at.core == 0)
        def _():
            b_twin(2, 1, p).start()

    each_piece(share)

    def finish(p):
        for step in range(STEPS):
            pltpu.make_async_copy(a_final(step, p), a_final(step, p), a_got.at[step, p]).wait()
        b_wait(1, p)
        b_wait(3, p)
        b_twin(0, 1, p).wait_send()

        @pl.when(at.core == 1)
        def _():
            b_twin(2, 3, p).wait_send()

        for turn in (1, 2, 3):
            a_spread(turn, p).wait_send()
        for step in (0, 2, 3):
            _, here, _ = at.b_peer(step)

            @pl.when(at.b_direct(step) & ~here)
            def _():
                b_spread(step, p).wait_send()

        for cond, copy in (
            (at.send1, lambda: a_direct(0, p)),
            (at.send2, lambda: a_direct(1, p)),
            (at.relay1, lambda: a_on(0, p)),
            (at.relay2, lambda: a_on(1, p)),
            (at.near, lambda: b_near(p)),
            (at.far, lambda: b_far(p)),
        ):

            @pl.when(cond)
            def _():
                copy().wait_send()

    each_piece(finish)


def move(a_blocks, b_blocks, a_coord, a_count, b_coord, b_count):
    pieces = NB + 1
    dma = pltpu.SemaphoreType.DMA
    panel = jax.ShapeDtypeStruct((STEPS, NB, BW, BW), jnp.bfloat16)
    table = jax.ShapeDtypeStruct((STEPS, 8, 128), jnp.int32)
    anywhere = pl.BlockSpec(memory_space=pl.ANY)
    scalars = pl.BlockSpec(memory_space=pltpu.SMEM)
    return pl.pallas_call(
        move_kernel,
        out_shape=[panel, panel, table, table],
        in_specs=[anywhere] * 2 + [scalars] * 4,
        out_specs=[anywhere] * 4,
        scratch_shapes=[
            pltpu.VMEM((2, NB, BW, BW), jnp.bfloat16),
            pltpu.VMEM((3, NB, BW, BW), jnp.bfloat16),
            pltpu.VMEM((8, 128), jnp.int32),
            pltpu.VMEM((8, 128), jnp.int32),
            pltpu.VMEM((2, 8, 128), jnp.int32),
            pltpu.VMEM((3, 8, 128), jnp.int32),
            dma((2, pieces)),
            dma((2, pieces)),
            dma((3, pieces)),
            dma((2, pieces)),
            dma((STEPS, pieces)),
            dma((2, pieces)),
            dma((2, pieces)),
            dma((3, pieces)),
            dma((STEPS, pieces)),
            dma((STEPS, pieces)),
            pltpu.SemaphoreType.REGULAR,
            pltpu.SemaphoreType.REGULAR,
            pltpu.SemaphoreType.REGULAR,
            pltpu.SemaphoreType.REGULAR,
        ],
        compiler_params=pltpu.CompilerParams(collective_id=0, has_side_effects=True),
    )(a_blocks, b_blocks, a_coord, a_count, b_coord, b_count)


def product_kernel(a_table, b_table, pattern, a_ref, b_ref, out_ref, total):
    total[...] = jnp.zeros_like(total)
    for step in range(STEPS):
        for slot in range(NB):
            code = a_table[step, 0, 16 + slot]

            @pl.when(code >= 0)
            def _():
                r, k = code // BR, code % BR
                blocks = []
                for c in range(BR):
                    which = b_table[step, 0, k * BR + c]
                    block = b_ref[step, jnp.minimum(which, NB - 1)]
                    kept = (which < NB) & (pattern[r, c] > 0)
                    blocks.append(jnp.where(kept, block, jnp.zeros_like(block)))
                row = jnp.concatenate(blocks, axis=1)
                total[r] += jnp.dot(a_ref[step, slot], row, preferred_element_type=jnp.float32)

    out_ref[...] = total[...].reshape(out_ref.shape).astype(out_ref.dtype)


def product(a_panels, b_panels, a_table, b_table, pattern):
    whole = pl.BlockSpec(memory_space=pltpu.VMEM)
    scalars = pl.BlockSpec(memory_space=pltpu.SMEM)
    span = BR * BW
    return pl.pallas_call(
        product_kernel,
        out_shape=jax.ShapeDtypeStruct((span, span), jnp.bfloat16),
        in_specs=[scalars] * 3 + [whole] * 2,
        out_specs=whole,
        scratch_shapes=[pltpu.VMEM((BR, BW, span), jnp.float32)],
    )(a_table, b_table, pattern, a_panels, b_panels)


def per_device(a_blocks, a_coord, a_count, b_blocks, b_coord, b_count, c_pattern):
    moved = move(a_blocks, b_blocks, a_coord, a_count, b_coord, b_count)
    return product(*moved, c_pattern)


def solution(mesh):
    placed = (
        P("row", "col", None),
        P("row", "col"),
        P("row", "col"),
        P("row", "col", None),
        P("row", "col"),
        P("row", "col"),
        P("row", "col"),
    )
    return jax.shard_map(
        per_device, mesh=mesh, in_specs=placed, out_specs=P("row", "col"), check_vma=False
    )
```

```python
import jax
import jax.numpy as jnp
from jax import lax
from jax.experimental import pallas as pl
from jax.experimental.pallas import tpu as pltpu
from jax.sharding import PartitionSpec as P

MESH = pl.DeviceIdType.MESH
STEPS = 4
NB = 4
BR = 4
BW = 128
DEAD = NB
NP = 4


class Place:
    def __init__(self):
        self.i = i = lax.axis_index("row")
        self.j = j = lax.axis_index("col")
        self.w, self.x = w, x = j // 4, j % 4
        self.zh, self.pos = zh, pos = i // 8, i % 8

        ahead = i - x
        d1, d2 = (ahead + 3) // 4, (ahead + 6) // 4
        self.two = two = d1 != d2
        self.ha = (x - i + 32) % 4
        self.z1, self.z2 = z1, z2 = (w + d1) % 8, (w + d2) % 8
        g1, g2 = (w - d1 + 16) % 8, (w - d2 + 16) % 8
        self.g1, self.g2 = g1, g2
        need1, need2 = g1 != w, two & (g2 != w)
        self.send1 = need1 & ~(need2 & (g1 > w))
        self.send2 = need2 & ~(need1 & (g1 < w) & (g1 > 0))
        self.own1, self.own2 = z1 == w, two & (z2 == w)
        self.in1 = (z1 != w) & ~(two & (w > z1) & (w - 1 != z1))
        self.in2 = two & (z2 != w) & ~((w + 1 <= 7) & (w + 1 < z2))
        self.late1 = (z1 != w) & ~self.in1
        self.late2 = two & (z2 != w) & ~self.in2
        self.relay1 = two & (w >= 1) & (w < z1)
        self.relay2 = two & (w <= 6) & (w > z2)

        e = j - pos
        self.hb = (pos - j + 32) % 8
        self.core, self.twin = pos % 2, (zh * 8 + pos + 1 - 2 * (pos % 2), j)
        down = ((e >= -2) & (e <= 8)) | (e >= 30)
        up = (e >= 14) & (e <= 24)
        self.near = near = down | up
        self.far = far = (e >= 6) & (e <= 16)
        self.near_to = jnp.where(down, (zh + 3) % 4, (zh + 1) % 4) * 8 + pos
        self.near_from = jnp.where(down, (zh + 1) % 4, (zh + 3) % 4) * 8 + pos
        self.far_to = ((zh + 2) % 4) * 8 + pos
        late = up & ~far
        greet_up = near & ((zh <= 1) | ((zh == 2) & ~late))
        greet_down = near & ((zh == 0) | ((zh == 3) & late))
        self.greet_to = jnp.where(down, greet_down, greet_up)
        self.greet_from = jnp.where(down, greet_up, greet_down)
        self.met_to, self.met_from = near & ~self.greet_to, near & ~self.greet_from
        self.far_send = far & (~near | (zh == 2))
        self.pass_on = near & far & (self.near_from // 8 != 2)
        alone = far & ~near
        self.far_send = self.far_send & ~(alone & (zh == 1))
        self.swap_send, self.swap_get = alone & (zh == 1), alone & (zh == 0)
        self.swap_to, self.swap_on = (1 - zh) * 8 + pos, 24 + pos
        self.swap_end = alone & (zh == 3)
        self.greet_far = far & ((zh == 0) | ((zh == 1) & ~near))
        self.met_far = far & ((zh == 2) | ((zh == 3) & ~near))
        self.told_far, self.tell_far = alone & (zh == 0), alone & (zh == 2)
        self.first = jnp.where((e <= 0) | (e >= 25), 0, jnp.where((e >= 9) & (e <= 16), 2, 1))
        self.second = jnp.where(
            (e <= -3) | ((e >= 22) & (e <= 29)), 0, jnp.where((e >= 6) & (e <= 13), 2, 1)
        )

    def a_peer(self, turn):
        xd = (self.x + turn) % 4
        step = (self.x - self.i - xd + 64) % 4
        slot = jnp.where(xd <= self.ha, 0, 1)
        return (self.i, self.w * 4 + xd), step, slot

    def a_step_from(self, turn):
        return ((self.x + turn) - self.i - self.x + 64) % 4

    def b_peer(self, step):
        pd = (self.pos - self.j - step + 64) % 8
        slot = jnp.where(step <= self.hb, self.first, self.second)
        return (self.zh * 8 + pd, self.j), pd == self.pos, slot

    def b_direct(self, step):
        return (self.pos - self.j) % 2 == 0 if step == 3 else step != 1

    def b_source(self, step):
        ps = (self.pos + self.j + step) % 8
        return (self.zh * 8 + ps, self.j)

    def z_peer(self, z):
        return (self.i, z * 4 + self.x)


def live_table(coord, count):
    lane = lax.broadcasted_iota(jnp.int32, (1, 128), 1)
    table = jnp.full((1, 128), DEAD, jnp.int32)
    for s in range(NB):
        live = s < count[0, 0]
        table = jnp.where((lane == coord[0, s]) & live, s, table)
        table = jnp.where(lane == 16 + s, jnp.where(live, coord[0, s], -1), table)
    return table


def move_kernel(
    a_ref, b_ref, a_coord, a_count, b_coord, b_count,
    a_out, b_out, a_table_out, b_table_out,
    a_buf, b_buf, a_own_table, b_own_table, a_table, b_table,
    a_send, a_relay, a_fan, b_send, b_fan, b_twins,
    a_have, b_have, a_got, b_got, near_ready, far_ready, swap_ready, below, above,
):
    at = Place()
    i, w = at.i, at.w

    a_own_table[...] = live_table(a_coord, a_count)
    b_own_table[...] = live_table(b_coord, b_count)

    def part(p):
        return pl.ds(p * (NB // NP), NB // NP)

    def a_own(p):
        return a_own_table if p is NB else a_ref.at[part(p)]

    def b_own(p):
        return b_own_table if p is NB else b_ref.at[part(p)]

    def a_slot(k, p):
        return a_table.at[k] if p is NB else a_buf.at[k, part(p)]

    def b_slot(k, p):
        return b_table.at[k] if p is NB else b_buf.at[k, part(p)]

    def a_final(s, p):
        return a_table_out.at[s] if p is NB else a_out.at[s, part(p)]

    def b_final(s, p):
        return b_table_out.at[s] if p is NB else b_out.at[s, part(p)]

    def remote(src, dst, send, recv, to):
        return pltpu.make_async_remote_copy(
            src_ref=src, dst_ref=dst, send_sem=send, recv_sem=recv, device_id=to, device_id_type=MESH
        )

    def a_direct(n, p):
        to = at.z_peer(at.g1 if n == 0 else at.g2)
        return remote(a_own(p), a_slot(n, p), a_send.at[n, p], a_have.at[n, p], to)

    def a_on(n, p):
        to = at.z_peer(at.w - 1 if n == 0 else at.w + 1)
        return remote(a_slot(n, p), a_slot(1 - n, p), a_relay.at[n, p], a_have.at[1 - n, p], to)

    def a_keep(n, p):
        return pltpu.make_async_copy(a_own(p), a_slot(n, p), a_have.at[n, p])

    def a_spread(turn, p):
        to, step, slot = at.a_peer(turn)
        if turn == 0:
            return pltpu.make_async_copy(a_slot(slot, p), a_final(step, p), a_got.at[step, p])
        return remote(a_slot(slot, p), a_final(step, p), a_fan.at[turn - 1, p], a_got.at[step, p], to)

    def b_near(p):
        return remote(b_own(p), b_slot(1, p), b_send.at[0, p], b_have.at[1, p], (at.near_to, at.j))

    def b_far(p):
        return remote(b_own(p), b_slot(2, p), b_send.at[1, p], b_have.at[2, p], (at.far_to, at.j))

    def b_pass(p):
        return remote(b_slot(1, p), b_slot(2, p), b_send.at[2, p], b_have.at[2, p], (at.near_to, at.j))

    def b_swap(p):
        return remote(b_own(p), b_slot(3, p), b_send.at[1, p], b_have.at[3, p], (at.swap_to, at.j))

    def b_swap_on(p):
        return remote(b_slot(3, p), b_slot(2, p), b_send.at[2, p], b_have.at[2, p], (at.swap_on, at.j))

    def b_keep(p):
        return pltpu.make_async_copy(b_own(p), b_slot(0, p), b_have.at[0, p])

    def b_spread(step, p):
        to, _, slot = at.b_peer(step)
        return remote(b_slot(slot, p), b_final(step, p), b_fan.at[step, p], b_got.at[step, p], to)

    def b_spread_here(step, p):
        _, _, slot = at.b_peer(step)
        return pltpu.make_async_copy(b_slot(slot, p), b_final(step, p), b_got.at[step, p])

    def b_twin(step, to, p):
        return remote(b_final(step, p), b_final(to, p), b_twins.at[to // 2, p], b_got.at[to, p], at.twin)

    def b_wait(step, p):
        pltpu.make_async_copy(b_final(step, p), b_final(step, p), b_got.at[step, p]).wait()

    barrier = pltpu.get_barrier_semaphore()

    def greet(device):
        pl.semaphore_signal(barrier, inc=1, device_id=device, device_id_type=MESH)

    def greet_if(cond, device):
        @pl.when(cond)
        def _():
            greet(device)

    def each_piece(body):
        body(NB)
        lax.fori_loop(0, NP, lambda p, c: (body(p), c)[1], 0)

    greet_if(w > 0, at.z_peer(w - 1))
    greet_if(w < 7, at.z_peer(w + 1))
    greet_if(at.greet_to, (at.near_to, at.j))
    greet_if(at.greet_from, (at.near_from, at.j))
    greet_if(at.greet_far, (at.far_to, at.j))
    greet_if(at.swap_get, (at.swap_to, at.j))
    greet_if(at.swap_get, (at.swap_on, at.j))
    for turn in (1, 2, 3):
        greet((i, w * 4 + (at.x + turn) % 4))
    greet(at.twin)
    away = jnp.int32(1)
    for step in (0, 2, 3):
        _, here, _ = at.b_peer(step)
        source = at.b_source(step)
        greet_if((source[0] != i) & ((at.core == 1) | (step != 3)), source)
        away = away + jnp.where(at.b_direct(step) & ~here, 1, 0)

    def keep(p):
        @pl.when(at.own1)
        def _():
            a_keep(0, p).start()

        @pl.when(at.own2)
        def _():
            a_keep(1, p).start()

        b_keep(p).start()

    each_piece(keep)

    def one(flag):
        return jnp.where(flag, 1, 0)

    pl.semaphore_wait(
        barrier,
        3 + away + one(w > 0) + one(w < 7) + one(at.met_to) + one(at.met_from) + one(at.met_far) + one(at.swap_send) + one(at.swap_end),
    )

    def leave_near(p):
        b_near(p).start()

    def leave_far(p):
        b_far(p).start()

    def leave_a(p):
        @pl.when(at.send1)
        def _():
            a_direct(0, p).start()

        @pl.when(at.send2)
        def _():
            a_direct(1, p).start()

    def spread_a(p, slot_ready):
        for turn in (1, 2, 3, 0):
            _, _, slot = at.a_peer(turn)

            @pl.when(jnp.where(slot == 0, slot_ready[0], slot_ready[1]))
            def _():
                a_spread(turn, p).start()

    def spread_b(p, ready):
        for step in (0, 2, 3):
            _, here, slot = at.b_peer(step)
            mine = ready(slot) & at.b_direct(step)

            @pl.when(mine & ~here)
            def _():
                b_spread(step, p).start()

            @pl.when(mine & here)
            def _():
                b_spread_here(step, p).start()

    early1, early2 = at.in1 | at.own1, at.in2 | at.own2

    def near_b(p):
        b_keep(p).wait()

        @pl.when(at.near)
        def _():
            b_near(p).wait_recv()

        @pl.when(at.pass_on)
        def _():
            b_pass(p).start()

        spread_b(p, lambda slot: slot <= 1)

    def relay_a(p):
        @pl.when(early1)
        def _():
            a_direct(0, p).wait_recv()

        @pl.when(at.relay1)
        def _():
            a_on(0, p).start()

        @pl.when(early2)
        def _():
            a_direct(1, p).wait_recv()

        @pl.when(at.relay2)
        def _():
            a_on(1, p).start()

        spread_a(p, (early1, early2))

    def late_a(p):
        @pl.when(at.late1)
        def _():
            a_direct(0, p).wait_recv()

        @pl.when(at.late2)
        def _():
            a_direct(1, p).wait_recv()

        spread_a(p, (at.late1, at.late2))

    def far_b(p):
        @pl.when(at.far)
        def _():
            b_far(p).wait_recv()

        spread_b(p, lambda slot: slot == 2)

    @pl.when(at.met_from)
    def _():
        pl.semaphore_signal(near_ready, inc=1, device_id=(at.near_from, at.j), device_id_type=MESH)

    @pl.when(at.swap_end)
    def _():
        pl.semaphore_signal(swap_ready, inc=1, device_id=(at.pos, at.j), device_id_type=MESH)

    @pl.when(at.tell_far)
    def _():
        pl.semaphore_signal(far_ready, inc=1, device_id=(at.far_to, at.j), device_id_type=MESH)

    @pl.when(at.far_send & (at.zh == 2))
    def _():
        each_piece(leave_far)

    @pl.when(at.met_to)
    def _():
        each_piece(leave_near)

    def leave_swap(p):
        b_swap(p).start()

    @pl.when(at.swap_send)
    def _():
        each_piece(leave_swap)

    @pl.when(at.far_send & (at.zh == 3))
    def _():
        each_piece(leave_far)

    def from_below():
        @pl.when(w > 0)
        def _():
            pl.semaphore_wait(below, 1)

        @pl.when(w < 7)
        def _():
            pl.semaphore_signal(below, inc=1, device_id=at.z_peer(w + 1), device_id_type=MESH)

    def from_above():
        @pl.when(w < 7)
        def _():
            pl.semaphore_wait(above, 1)

        @pl.when(w > 0)
        def _():
            pl.semaphore_signal(above, inc=1, device_id=at.z_peer(w - 1), device_id_type=MESH)

    @pl.when(w < 4)
    def _():
        from_below()
        from_above()

    @pl.when(w >= 4)
    def _():
        from_above()
        from_below()

    each_piece(leave_a)
    a_first = at.zh == 0

    @pl.when(a_first)
    def _():
        each_piece(relay_a)
        each_piece(late_a)

    @pl.when(at.greet_to)
    def _():
        pl.semaphore_wait(near_ready, 1)
        each_piece(leave_near)

    def swap_on(p):
        b_swap(p).wait_recv()
        b_swap_on(p).start()

    @pl.when(at.swap_get)
    def _():
        pl.semaphore_wait(swap_ready, 1)
        each_piece(swap_on)

    @pl.when(at.told_far)
    def _():
        pl.semaphore_wait(far_ready, 1)
        each_piece(leave_far)

    each_piece(near_b)

    @pl.when(~a_first)
    def _():
        each_piece(relay_a)
        each_piece(late_a)

    each_piece(far_b)

    def share(p):
        b_wait(0, p)

        @pl.when(at.core == 1)
        def _():
            b_twin(0, 1, p).start()

        b_wait(2, p)

        @pl.when(at.core == 1)
        def _():
            b_twin(2, 3, p).start()

        @pl.when(at.core == 0)
        def _():
            b_twin(2, 1, p).start()

    each_piece(share)

    def finish(p):
        for step in range(STEPS):
            pltpu.make_async_copy(a_final(step, p), a_final(step, p), a_got.at[step, p]).wait()
        b_wait(1, p)
        b_wait(3, p)
        b_twin(0, 1, p).wait_send()

        @pl.when(at.core == 1)
        def _():
            b_twin(2, 3, p).wait_send()

        for turn in (1, 2, 3):
            a_spread(turn, p).wait_send()
        for step in (0, 2, 3):
            _, here, _ = at.b_peer(step)

            @pl.when(at.b_direct(step) & ~here)
            def _():
                b_spread(step, p).wait_send()

        for cond, copy in (
            (at.send1, lambda: a_direct(0, p)),
            (at.send2, lambda: a_direct(1, p)),
            (at.relay1, lambda: a_on(0, p)),
            (at.relay2, lambda: a_on(1, p)),
            (at.near, lambda: b_near(p)),
            (at.far_send, lambda: b_far(p)),
            (at.pass_on, lambda: b_pass(p)),
            (at.swap_send, lambda: b_swap(p)),
            (at.swap_get, lambda: b_swap_on(p)),
        ):

            @pl.when(cond)
            def _():
                copy().wait_send()

    each_piece(finish)


def move(a_blocks, b_blocks, a_coord, a_count, b_coord, b_count):
    pieces = NB + 1
    dma = pltpu.SemaphoreType.DMA
    panel = jax.ShapeDtypeStruct((STEPS, NB, BW, BW), jnp.bfloat16)
    table = jax.ShapeDtypeStruct((STEPS, 1, 128), jnp.int32)
    anywhere = pl.BlockSpec(memory_space=pl.ANY)
    scalars = pl.BlockSpec(memory_space=pltpu.SMEM)
    return pl.pallas_call(
        move_kernel,
        out_shape=[panel, panel, table, table],
        in_specs=[anywhere] * 2 + [scalars] * 4,
        out_specs=[anywhere] * 4,
        scratch_shapes=[
            pltpu.VMEM((2, NB, BW, BW), jnp.bfloat16),
            pltpu.VMEM((4, NB, BW, BW), jnp.bfloat16),
            pltpu.VMEM((1, 128), jnp.int32),
            pltpu.VMEM((1, 128), jnp.int32),
            pltpu.VMEM((2, 1, 128), jnp.int32),
            pltpu.VMEM((4, 1, 128), jnp.int32),
            dma((2, pieces)),
            dma((2, pieces)),
            dma((3, pieces)),
            dma((3, pieces)),
            dma((STEPS, pieces)),
            dma((2, pieces)),
            dma((2, pieces)),
            dma((4, pieces)),
            dma((STEPS, pieces)),
            dma((STEPS, pieces)),
            pltpu.SemaphoreType.REGULAR,
            pltpu.SemaphoreType.REGULAR,
            pltpu.SemaphoreType.REGULAR,
            pltpu.SemaphoreType.REGULAR,
            pltpu.SemaphoreType.REGULAR,
        ],
        compiler_params=pltpu.CompilerParams(collective_id=0, has_side_effects=True),
    )(a_blocks, b_blocks, a_coord, a_count, b_coord, b_count)


def product_kernel(a_table, b_table, pattern, a_ref, b_ref, out_ref, total):
    total[...] = jnp.zeros_like(total)
    for step in range(STEPS):
        for slot in range(NB):
            code = a_table[step, 0, 16 + slot]
            r, k = jnp.maximum(code, 0) // BR, jnp.maximum(code, 0) % BR
            which = [b_table[step, 0, k * BR + c] for c in range(BR)]
            kept = [(which[c] < NB) & (pattern[r, c] > 0) for c in range(BR)]

            @pl.when((code >= 0) & (kept[0] | kept[1] | kept[2] | kept[3]))
            def _():
                blocks = []
                for c in range(BR):
                    block = b_ref[step, jnp.minimum(which[c], NB - 1)]
                    blocks.append(jnp.where(kept[c], block, jnp.zeros_like(block)))
                row = jnp.concatenate(blocks, axis=1)
                total[r] += jnp.dot(a_ref[step, slot], row, preferred_element_type=jnp.float32)

    out_ref[...] = total[...].reshape(out_ref.shape).astype(out_ref.dtype)


def product(a_panels, b_panels, a_table, b_table, pattern):
    whole = pl.BlockSpec(memory_space=pltpu.VMEM)
    scalars = pl.BlockSpec(memory_space=pltpu.SMEM)
    span = BR * BW
    return pl.pallas_call(
        product_kernel,
        out_shape=jax.ShapeDtypeStruct((span, span), jnp.bfloat16),
        in_specs=[scalars] * 3 + [whole] * 2,
        out_specs=whole,
        scratch_shapes=[pltpu.VMEM((BR, BW, span), jnp.float32)],
    )(a_table, b_table, pattern, a_panels, b_panels)


def per_device(a_blocks, a_coord, a_count, b_blocks, b_coord, b_count, c_pattern):
    moved = move(a_blocks, b_blocks, a_coord, a_count, b_coord, b_count)
    return product(*moved, c_pattern)


def solution(mesh):
    placed = (
        P("row", "col", None),
        P("row", "col"),
        P("row", "col"),
        P("row", "col", None),
        P("row", "col"),
        P("row", "col"),
        P("row", "col"),
    )
    return jax.shard_map(
        per_device, mesh=mesh, in_specs=placed, out_specs=P("row", "col"), check_vma=False
    )
```

```python
import jax
import jax.numpy as jnp
from jax import lax
from jax.experimental import pallas as pl
from jax.experimental.pallas import tpu as pltpu
from jax.sharding import PartitionSpec as P

MESH = pl.DeviceIdType.MESH
STEPS = 4
NB = 4
BR = 4
BW = 128
DEAD = NB
NP = 4


class Place:
    def __init__(self):
        self.i = i = lax.axis_index("row")
        self.j = j = lax.axis_index("col")
        self.w, self.x = w, x = j // 4, j % 4
        self.zh, self.pos = zh, pos = i // 8, i % 8

        ahead = i - x
        d1, d2 = (ahead + 3) // 4, (ahead + 6) // 4
        self.two = two = d1 != d2
        self.ha = (x - i + 32) % 4
        self.z1, self.z2 = z1, z2 = (w + d1) % 8, (w + d2) % 8
        g1, g2 = (w - d1 + 16) % 8, (w - d2 + 16) % 8
        self.g1, self.g2 = g1, g2
        need1, need2 = g1 != w, two & (g2 != w)
        self.send1 = need1 & ~(need2 & (g1 > w))
        self.send2 = need2 & ~(need1 & (g1 < w) & (g1 > 0))
        self.own1, self.own2 = z1 == w, two & (z2 == w)
        self.in1 = (z1 != w) & ~(two & (w > z1) & (w - 1 != z1))
        self.in2 = two & (z2 != w) & ~((w + 1 <= 7) & (w + 1 < z2))
        self.late1 = (z1 != w) & ~self.in1
        self.late2 = two & (z2 != w) & ~self.in2
        self.relay1 = two & (w >= 1) & (w < z1)
        self.relay2 = two & (w <= 6) & (w > z2)

        e = j - pos
        self.hb = (pos - j + 32) % 8
        self.core, self.twin = pos % 2, (zh * 8 + pos + 1 - 2 * (pos % 2), j)
        down = ((e >= -2) & (e <= 8)) | (e >= 30)
        up = (e >= 14) & (e <= 24)
        self.near = near = down | up
        self.far = far = (e >= 6) & (e <= 16)
        self.near_to = jnp.where(down, (zh + 3) % 4, (zh + 1) % 4) * 8 + pos
        self.near_from = jnp.where(down, (zh + 1) % 4, (zh + 3) % 4) * 8 + pos
        self.far_to = ((zh + 2) % 4) * 8 + pos
        late = up
        greet_up = near & ((zh <= 1) | ((zh == 2) & ~late))
        greet_down = near & ((zh == 0) | ((zh == 3) & late))
        self.greet_to = jnp.where(down, greet_down, greet_up)
        self.greet_from = jnp.where(down, greet_up, greet_down)
        self.met_to, self.met_from = near & ~self.greet_to, near & ~self.greet_from
        self.far_send = far & ~near
        self.pass_on = near & far
        alone = far & ~near
        self.far_send = self.far_send & ~(alone & (zh == 1))
        self.swap_send, self.swap_get = alone & (zh == 1), alone & (zh == 0)
        self.swap_to, self.swap_on = (1 - zh) * 8 + pos, 24 + pos
        self.swap_end = alone & (zh == 3)
        self.greet_far = far & ((zh == 0) | ((zh == 1) & ~near))
        self.met_far = far & ((zh == 2) | ((zh == 3) & ~near))
        self.told_far, self.tell_far = alone & (zh == 0), alone & (zh == 2)
        self.first = jnp.where((e <= 0) | (e >= 25), 0, jnp.where((e >= 9) & (e <= 16), 2, 1))
        self.second = jnp.where(
            (e <= -3) | ((e >= 22) & (e <= 29)), 0, jnp.where((e >= 6) & (e <= 13), 2, 1)
        )

    def a_peer(self, turn):
        xd = (self.x + turn) % 4
        step = (self.x - self.i - xd + 64) % 4
        slot = jnp.where(xd <= self.ha, 0, 1)
        return (self.i, self.w * 4 + xd), step, slot

    def a_step_from(self, turn):
        return ((self.x + turn) - self.i - self.x + 64) % 4

    def b_peer(self, step):
        pd = (self.pos - self.j - step + 64) % 8
        slot = jnp.where(step <= self.hb, self.first, self.second)
        return (self.zh * 8 + pd, self.j), pd == self.pos, slot

    def b_direct(self, step):
        return (self.pos - self.j) % 2 == 0 if step == 3 else step != 1

    def b_source(self, step):
        ps = (self.pos + self.j + step) % 8
        return (self.zh * 8 + ps, self.j)

    def z_peer(self, z):
        return (self.i, z * 4 + self.x)


def live_table(coord, count):
    lane = lax.broadcasted_iota(jnp.int32, (1, 128), 1)
    table = jnp.full((1, 128), DEAD, jnp.int32)
    for s in range(NB):
        live = s < count[0, 0]
        table = jnp.where((lane == coord[0, s]) & live, s, table)
        table = jnp.where(lane == 16 + s, jnp.where(live, coord[0, s], -1), table)
    return table


def move_kernel(
    a_ref, b_ref, a_coord, a_count, b_coord, b_count,
    a_out, b_out, a_table_out, b_table_out,
    a_buf, b_buf, a_own_table, b_own_table, a_table, b_table,
    a_send, a_relay, a_fan, b_send, b_fan, b_twins,
    a_have, b_have, a_got, b_got, near_ready, far_ready, swap_ready, below, above,
):
    at = Place()
    i, w = at.i, at.w

    def part(p):
        return pl.ds(p * (NB // NP), NB // NP) if isinstance(p, (int, jax.Array)) else p

    def a_own(p):
        return a_own_table if p is NB else a_ref.at[part(p)]

    def b_own(p):
        return b_own_table if p is NB else b_ref.at[part(p)]

    def a_slot(k, p):
        return a_table.at[k] if p is NB else a_buf.at[k, part(p)]

    def b_slot(k, p):
        return b_table.at[k] if p is NB else b_buf.at[k, part(p)]

    def a_final(s, p):
        return a_table_out.at[s] if p is NB else a_out.at[s, part(p)]

    def b_final(s, p):
        return b_table_out.at[s] if p is NB else b_out.at[s, part(p)]

    def remote(src, dst, send, recv, to):
        return pltpu.make_async_remote_copy(
            src_ref=src, dst_ref=dst, send_sem=send, recv_sem=recv, device_id=to, device_id_type=MESH
        )

    def whole(p):
        return 1 if p is NB else 0

    def a_direct(n, p):
        to = at.z_peer(at.g1 if n == 0 else at.g2)
        return remote(a_own(p), a_slot(n, p), a_send.at[n, whole(p)], a_have.at[n, p], to)

    def a_on(n, p):
        to = at.z_peer(at.w - 1 if n == 0 else at.w + 1)
        return remote(a_slot(n, p), a_slot(1 - n, p), a_relay.at[n, whole(p)], a_have.at[1 - n, p], to)

    def a_keep(n, p):
        return pltpu.make_async_copy(a_own(p), a_slot(n, p), a_have.at[n, p])

    def a_spread(turn, p):
        to, step, slot = at.a_peer(turn)
        if turn == 0:
            return pltpu.make_async_copy(a_slot(slot, p), a_final(step, p), a_got.at[step, whole(p)])
        return remote(a_slot(slot, p), a_final(step, p), a_fan.at[turn - 1, whole(p)], a_got.at[step, whole(p)], to)

    def b_near(p):
        return remote(b_own(p), b_slot(1, p), b_send.at[0, whole(p)], b_have.at[1, p], (at.near_to, at.j))

    def b_far(p):
        return remote(b_own(p), b_slot(2, p), b_send.at[1, whole(p)], b_have.at[2, p], (at.far_to, at.j))

    def b_pass(p):
        return remote(b_slot(1, p), b_slot(2, p), b_send.at[2, whole(p)], b_have.at[2, p], (at.near_to, at.j))

    def b_swap(p):
        return remote(b_own(p), b_slot(3, p), b_send.at[1, whole(p)], b_have.at[3, p], (at.swap_to, at.j))

    def b_swap_on(p):
        return remote(b_slot(3, p), b_slot(2, p), b_send.at[2, whole(p)], b_have.at[2, p], (at.swap_on, at.j))

    def b_keep(p):
        return pltpu.make_async_copy(b_own(p), b_slot(0, p), b_have.at[0, p])

    def b_spread(step, p):
        to, _, slot = at.b_peer(step)
        return remote(b_slot(slot, p), b_final(step, p), b_fan.at[step, whole(p)], b_got.at[step, p], to)

    def b_spread_here(step, p):
        _, _, slot = at.b_peer(step)
        return pltpu.make_async_copy(b_slot(slot, p), b_final(step, p), b_got.at[step, p])

    def b_twin(step, to, p):
        return remote(b_final(step, p), b_final(to, p), b_twins.at[to // 2, whole(p)], b_got.at[to, p], at.twin)

    def b_wait(step, p):
        pltpu.make_async_copy(b_final(step, p), b_final(step, p), b_got.at[step, p]).wait()

    def b_wait_whole(step, p):
        for q in (NB,) if p is NB else range(NP):
            b_wait(step, q)

    barrier = pltpu.get_barrier_semaphore()

    def greet(device):
        pl.semaphore_signal(barrier, inc=1, device_id=device, device_id_type=MESH)

    def greet_if(cond, device):
        @pl.when(cond)
        def _():
            greet(device)

    def each_piece(body):
        body(NB)
        lax.fori_loop(0, NP, lambda p, c: (body(p), c)[1], 0)

    greet_if(w > 0, at.z_peer(w - 1))
    greet_if(w < 7, at.z_peer(w + 1))
    greet_if(at.greet_to, (at.near_to, at.j))
    greet_if(at.greet_from, (at.near_from, at.j))
    greet_if(at.greet_far, (at.far_to, at.j))
    greet_if(at.swap_get, (at.swap_to, at.j))
    greet_if(at.swap_get, (at.swap_on, at.j))
    for turn in (1, 2, 3):
        greet((i, w * 4 + (at.x + turn) % 4))
    greet(at.twin)
    away = jnp.int32(1)
    for step in (0, 2, 3):
        _, here, _ = at.b_peer(step)
        source = at.b_source(step)
        greet_if((source[0] != i) & ((at.core == 1) | (step != 3)), source)
        away = away + jnp.where(at.b_direct(step) & ~here, 1, 0)

    a_own_table[...] = live_table(a_coord, a_count)
    b_own_table[...] = live_table(b_coord, b_count)

    def keep(p):
        @pl.when(at.own1)
        def _():
            a_keep(0, p).start()

        @pl.when(at.own2)
        def _():
            a_keep(1, p).start()

        b_keep(p).start()

    each_piece(keep)

    def one(flag):
        return jnp.where(flag, 1, 0)

    pl.semaphore_wait(
        barrier,
        3 + away + one(w > 0) + one(w < 7) + one(at.met_to) + one(at.met_from) + one(at.met_far) + one(at.swap_send) + one(at.swap_end),
    )

    def leave_near(p):
        b_near(p).start()

    def leave_far(p):
        b_far(p).start()

    def leave_a(p, low, high):
        @pl.when(at.send1 & jnp.where(at.g1 < w, low, high))
        def _():
            a_direct(0, p).start()

        @pl.when(at.send2 & jnp.where(at.g2 < w, low, high))
        def _():
            a_direct(1, p).start()

    def spread_a(p, slot_ready):
        for turn in (1, 2, 3, 0):
            _, _, slot = at.a_peer(turn)

            @pl.when(jnp.where(slot == 0, slot_ready[0], slot_ready[1]))
            def _():
                a_spread(turn, p).start()

    def spread_b(p, ready):
        for step in (0, 2, 3):
            _, here, slot = at.b_peer(step)
            mine = ready(slot) & at.b_direct(step)

            @pl.when(mine & ~here)
            def _():
                b_spread(step, p).start()

            @pl.when(mine & here)
            def _():
                b_spread_here(step, p).start()

    early1, early2 = at.in1 | at.own1, at.in2 | at.own2

    def near_b(p):
        b_keep(p).wait()

        @pl.when(at.near)
        def _():
            b_near(p).wait_recv()

        @pl.when(at.pass_on)
        def _():
            b_pass(p).start()

        spread_b(p, lambda slot: slot <= 1)

    def relay_a(p):
        @pl.when(early1)
        def _():
            a_direct(0, p).wait_recv()

        @pl.when(at.relay1)
        def _():
            a_on(0, p).start()

        @pl.when(early2)
        def _():
            a_direct(1, p).wait_recv()

        @pl.when(at.relay2)
        def _():
            a_on(1, p).start()

        spread_a(p, (early1, early2))

    def late_a(p):
        @pl.when(at.late1)
        def _():
            a_direct(0, p).wait_recv()

        @pl.when(at.late2)
        def _():
            a_direct(1, p).wait_recv()

        spread_a(p, (at.late1, at.late2))

    def far_b(p):
        @pl.when(at.far)
        def _():
            b_far(p).wait_recv()

        spread_b(p, lambda slot: slot == 2)

    @pl.when(at.met_from)
    def _():
        pl.semaphore_signal(near_ready, inc=1, device_id=(at.near_from, at.j), device_id_type=MESH)

    @pl.when(at.swap_end)
    def _():
        pl.semaphore_signal(swap_ready, inc=1, device_id=(at.pos, at.j), device_id_type=MESH)

    @pl.when(at.tell_far)
    def _():
        pl.semaphore_signal(far_ready, inc=1, device_id=(at.far_to, at.j), device_id_type=MESH)

    @pl.when(at.far_send & (at.zh == 2))
    def _():
        each_piece(leave_far)

    @pl.when(at.met_to)
    def _():
        each_piece(leave_near)

    def leave_swap(p):
        b_swap(p).start()

    @pl.when(at.swap_send)
    def _():
        each_piece(leave_swap)

    @pl.when(at.far_send & (at.zh == 3))
    def _():
        each_piece(leave_far)

    def from_below():
        @pl.when(w > 0)
        def _():
            pl.semaphore_wait(below, 1)

        @pl.when(w < 7)
        def _():
            pl.semaphore_signal(below, inc=1, device_id=at.z_peer(w + 1), device_id_type=MESH)

    def from_above():
        @pl.when(w < 7)
        def _():
            pl.semaphore_wait(above, 1)

        @pl.when(w > 0)
        def _():
            pl.semaphore_signal(above, inc=1, device_id=at.z_peer(w - 1), device_id_type=MESH)

    rising = (at.zh == 1) & (w <= 4)

    @pl.when(rising)
    def _():
        from_below()
        each_piece(lambda p: leave_a(p, True, False))
        from_above()
        each_piece(lambda p: leave_a(p, False, True))

    @pl.when(~rising)
    def _():
        @pl.when(w < 4)
        def _():
            from_below()
            from_above()

        @pl.when(w >= 4)
        def _():
            from_above()
            from_below()

        each_piece(lambda p: leave_a(p, True, True))

    a_first = at.zh == 0

    @pl.when(a_first)
    def _():
        each_piece(relay_a)
        each_piece(late_a)

    @pl.when(at.greet_to)
    def _():
        pl.semaphore_wait(near_ready, 1)
        each_piece(leave_near)

    def swap_on(p):
        b_swap(p).wait_recv()
        b_swap_on(p).start()

    @pl.when(at.swap_get)
    def _():
        pl.semaphore_wait(swap_ready, 1)
        each_piece(swap_on)

    @pl.when(at.told_far)
    def _():
        pl.semaphore_wait(far_ready, 1)
        each_piece(leave_far)

    each_piece(near_b)

    @pl.when(~a_first)
    def _():
        each_piece(relay_a)
        each_piece(late_a)

    each_piece(far_b)

    def share(p):
        b_wait(0, p)

        @pl.when(at.core == 1)
        def _():
            b_twin(0, 1, p).start()

        b_wait(2, p)

        @pl.when(at.core == 1)
        def _():
            b_twin(2, 3, p).start()

        @pl.when(at.core == 0)
        def _():
            b_twin(2, 1, p).start()

    each_piece(share)

    def finish(p):
        def all_of(ref):
            return ref(p) if p is NB else ref(pl.ds(0, NB))

        def wait(ref, sem):
            pltpu.make_async_copy(all_of(ref), all_of(ref), sem).wait()

        k = whole(p)
        for step in range(STEPS):
            wait(lambda q: a_final(step, q), a_got.at[step, k])
        b_wait_whole(1, p)
        b_wait_whole(3, p)

        def gone(sem):
            wait(a_own, sem)

        gone(b_twins.at[0, k])

        @pl.when(at.core == 1)
        def _():
            gone(b_twins.at[1, k])

        for turn in (1, 2, 3):
            gone(a_fan.at[turn - 1, k])
        for step in (0, 2, 3):
            _, here, _ = at.b_peer(step)

            @pl.when(at.b_direct(step) & ~here)
            def _():
                gone(b_fan.at[step, k])

        for cond, sem in (
            (at.send1, a_send.at[0, k]),
            (at.send2, a_send.at[1, k]),
            (at.relay1, a_relay.at[0, k]),
            (at.relay2, a_relay.at[1, k]),
            (at.near, b_send.at[0, k]),
            (at.far_send, b_send.at[1, k]),
            (at.pass_on, b_send.at[2, k]),
            (at.swap_send, b_send.at[1, k]),
            (at.swap_get, b_send.at[2, k]),
        ):

            @pl.when(cond)
            def _():
                gone(sem)

    finish(0)
    finish(NB)


def move(a_blocks, b_blocks, a_coord, a_count, b_coord, b_count):
    pieces = NB + 1
    dma = pltpu.SemaphoreType.DMA
    panel = jax.ShapeDtypeStruct((STEPS, NB, BW, BW), jnp.bfloat16)
    table = jax.ShapeDtypeStruct((STEPS, 1, 128), jnp.int32)
    anywhere = pl.BlockSpec(memory_space=pl.ANY)
    scalars = pl.BlockSpec(memory_space=pltpu.SMEM)
    return pl.pallas_call(
        move_kernel,
        out_shape=[panel, panel, table, table],
        in_specs=[anywhere] * 2 + [scalars] * 4,
        out_specs=[anywhere] * 4,
        scratch_shapes=[
            pltpu.VMEM((2, NB, BW, BW), jnp.bfloat16),
            pltpu.VMEM((4, NB, BW, BW), jnp.bfloat16),
            pltpu.VMEM((1, 128), jnp.int32),
            pltpu.VMEM((1, 128), jnp.int32),
            pltpu.VMEM((2, 1, 128), jnp.int32),
            pltpu.VMEM((4, 1, 128), jnp.int32),
            dma((2, pieces)),
            dma((2, pieces)),
            dma((3, pieces)),
            dma((3, pieces)),
            dma((STEPS, pieces)),
            dma((2, pieces)),
            dma((2, pieces)),
            dma((4, pieces)),
            dma((STEPS, pieces)),
            dma((STEPS, pieces)),
            pltpu.SemaphoreType.REGULAR,
            pltpu.SemaphoreType.REGULAR,
            pltpu.SemaphoreType.REGULAR,
            pltpu.SemaphoreType.REGULAR,
            pltpu.SemaphoreType.REGULAR,
        ],
        compiler_params=pltpu.CompilerParams(collective_id=0, has_side_effects=True),
    )(a_blocks, b_blocks, a_coord, a_count, b_coord, b_count)


def product_kernel(a_table, b_table, pattern, a_ref, b_ref, out_ref, total):
    total[...] = jnp.zeros_like(total)
    for step in range(STEPS):
        for slot in range(NB):
            code = a_table[step, 0, 16 + slot]
            r, k = jnp.maximum(code, 0) // BR, jnp.maximum(code, 0) % BR
            which = [b_table[step, 0, k * BR + c] for c in range(BR)]
            kept = [(which[c] < NB) & (pattern[r, c] > 0) for c in range(BR)]

            @pl.when((code >= 0) & (kept[0] | kept[1] | kept[2] | kept[3]))
            def _():
                blocks = []
                for c in range(BR):
                    block = b_ref[step, jnp.minimum(which[c], NB - 1)]
                    blocks.append(jnp.where(kept[c], block, jnp.zeros_like(block)))
                row = jnp.concatenate(blocks, axis=1)
                total[r] += jnp.dot(a_ref[step, slot], row, preferred_element_type=jnp.float32)

    out_ref[...] = total[...].reshape(out_ref.shape).astype(out_ref.dtype)


def product(a_panels, b_panels, a_table, b_table, pattern):
    whole = pl.BlockSpec(memory_space=pltpu.VMEM)
    scalars = pl.BlockSpec(memory_space=pltpu.SMEM)
    span = BR * BW
    return pl.pallas_call(
        product_kernel,
        out_shape=jax.ShapeDtypeStruct((span, span), jnp.bfloat16),
        in_specs=[scalars] * 3 + [whole] * 2,
        out_specs=whole,
        scratch_shapes=[pltpu.VMEM((BR, BW, span), jnp.float32)],
    )(a_table, b_table, pattern, a_panels, b_panels)


def per_device(a_blocks, a_coord, a_count, b_blocks, b_coord, b_count, c_pattern):
    moved = move(a_blocks, b_blocks, a_coord, a_count, b_coord, b_count)
    return product(*moved, c_pattern)


def solution(mesh):
    placed = (
        P("row", "col", None),
        P("row", "col"),
        P("row", "col"),
        P("row", "col", None),
        P("row", "col"),
        P("row", "col"),
        P("row", "col"),
    )
    return jax.shard_map(
        per_device, mesh=mesh, in_specs=placed, out_specs=P("row", "col"), check_vma=False
    )
```
